32 devices in a mesh: row: 4 (over y, x), col: 8 (over z, core).
Axes of the slice: x: 2, y: 2, z: 4, core: 2. Of those that a mesh axis runs over, the one named last changes fastest.
Arguments:
- resid_in: bfloat16 [1024, 4096], P('col', 'row'), may hold values from -6 to 6
- attn_out: bfloat16 [1024, 4096], P('row', 'col'), may hold values from -6 to 6
- cotangent: bfloat16 [1024, 4096], P('col', 'row'), may hold values from -6 to 6
- w_out: bfloat16 [4096, 4096], P('col', 'row'), may hold values from -0.09375 to 0.09375
- w_gate: bfloat16 [4096, 16384], P('row', 'col'), may hold values from -0.09375 to 0.09375
- w_up: bfloat16 [4096, 16384], P('row', 'col'), may hold values from -0.09375 to 0.09375
- w_down: bfloat16 [16384, 4096], P('col', 'row'), may hold values from -0.046875 to 0.046875
- mask_out: int32 [32, 32], P('col', 'row'), may hold values 0 or 1
- mask_gate: int32 [32, 128], P('row', 'col'), may hold values 0 or 1
- mask_up: int32 [32, 128], P('row', 'col'), may hold values 0 or 1
- mask_down: int32 [128, 32], P('col', 'row'), may hold values 0 or 1
Outputs:
- layer_out: bfloat16 [1024, 4096], P('col', 'row')
- grad_resid: bfloat16 [1024, 4096], P('col', 'row')
- grad_attn: bfloat16 [1024, 4096], P('row', 'col')
- grad_w_out: bfloat16 [4096, 4096], P('col', 'row')
- grad_w_gate: bfloat16 [4096, 16384], P('row', 'col')
- grad_w_up: bfloat16 [4096, 16384], P('row', 'col')
- grad_w_down: bfloat16 [16384, 4096], P('col', 'row')
The draws below stay inside these ranges and needn't reach their ends.
All inputs are finite; a program needn't handle non-finite values. No bound on the sum of `mask_out` or of `mask_gate` or of `mask_up` or of `mask_down` on one device may be relied on, other than what follows from the above.
Results may differ from the reference program's by a relative error of at most 0.0068.
Values may be sent and summed in bfloat16 or wider, within the bound.
A program may use at most 192 MiB of HBM per device.

```python
import jax
import jax.numpy as jnp

D = 4096
FF = 16384
BLOCK = 128
TOKENS = 1024


def place_ends(array, key, least, top_value):
    longest = array.shape.index(max(array.shape))
    spots = []
    for shift in (0, 1):
        where = [jax.random.randint(jax.random.fold_in(key, axis), (), 0, length) for axis, length in enumerate(array.shape)]
        where[longest] = (where[longest] + shift) % array.shape[longest]
        spots.append(tuple(where))
    return array.at[spots[0]].set(least).at[spots[1]].set(top_value)


def block_scale(own_key, dims, pieces, smallest, high):
    def one(dim, shards_of):
        heights = jax.random.uniform(jax.random.fold_in(jax.random.fold_in(own_key, 6), dim), (shards_of,), jnp.float32, smallest / len(pieces), high / len(pieces))
        return jnp.repeat(jnp.exp(heights), dims[dim] // shards_of).reshape((-1,) + (1,) * (len(dims) - dim - 1))

    gain = one(*pieces[0])
    for cut in pieces[1:]:
        gain = gain * one(*cut)
    return gain


def scatter_about(rng, extent, deviation, reach, shards=(), held_as=jnp.bfloat16):
    result = jax.random.normal(rng, extent, jnp.float32) * deviation
    if len(shards) > 0:
        result = block_scale(rng, extent, shards, -0.22, 0.18) * result
    return jnp.clip(result, min=-reach, max=reach).astype(held_as)


def setup_inputs(seed: int = 0) -> dict:
    splits = jax.random.split(jax.random.key(seed), 12)
    return {
        "resid_in": scatter_about(splits[0], (TOKENS, D), 1.0, 6.0, ((0, 8), (1, 4))),
        "attn_out": scatter_about(splits[1], (TOKENS, D), 1.0, 6.0, ((0, 4), (1, 8))),
        "cotangent": scatter_about(splits[2], (TOKENS, D), 1.0, 6.0, ((0, 8), (1, 4))),
        "w_out": scatter_about(splits[3], (D, D), D ** -0.5, 0.09375, ((0, 8), (1, 4))),
        "w_gate": scatter_about(splits[4], (D, FF), D ** -0.5, 0.09375, ((0, 4), (1, 8))),
        "w_up": scatter_about(splits[5], (D, FF), D ** -0.5, 0.09375, ((0, 4), (1, 8))),
        "w_down": scatter_about(splits[6], (FF, D), FF ** -0.5, 0.046875, ((0, 8), (1, 4))),
        "mask_out": place_ends((jax.random.randint(splits[7], (D // BLOCK, D // BLOCK), 0, 4) < 3).astype(jnp.int32), jax.random.fold_in(splits[7], 1), 0, 1),
        "mask_gate": place_ends((jax.random.randint(splits[8], (D // BLOCK, FF // BLOCK), 0, 4) < 3).astype(jnp.int32), jax.random.fold_in(splits[8], 1), 0, 1),
        "mask_up": place_ends((jax.random.randint(splits[9], (D // BLOCK, FF // BLOCK), 0, 4) < 3).astype(jnp.int32), jax.random.fold_in(splits[9], 1), 0, 1),
        "mask_down": place_ends((jax.random.randint(splits[10], (FF // BLOCK, D // BLOCK), 0, 4) < 3).astype(jnp.int32), jax.random.fold_in(splits[10], 1), 0, 1),
    }


def expand(weight, flags):
    blocks_r = weight.shape[0] // BLOCK
    blocks_c = weight.shape[1] // BLOCK
    shaped = weight.reshape(blocks_r, BLOCK, blocks_c, BLOCK)
    return (shaped * flags.astype(weight.dtype)[:, None, :, None]).reshape(weight.shape)


def reference(resid_in, attn_out, cotangent, w_out, w_gate, w_up, w_down, mask_out, mask_gate, mask_up, mask_down):
    f32 = jnp.float32
    pruned_out = expand(w_out, mask_out)
    pruned_gate = expand(w_gate, mask_gate)
    pruned_up = expand(w_up, mask_up)
    pruned_down = expand(w_down, mask_down)
    resid = (resid_in.astype(f32) + jnp.dot(attn_out, pruned_out, preferred_element_type=f32)).astype(jnp.bfloat16)
    gate_val = jnp.dot(resid, pruned_gate, preferred_element_type=f32)
    up_val = jnp.dot(resid, pruned_up, preferred_element_type=f32)
    logistic = jax.nn.sigmoid(gate_val)
    hidden = (gate_val * logistic * up_val).astype(jnp.bfloat16)
    layer_out = (resid.astype(f32) + jnp.dot(hidden, pruned_down, preferred_element_type=f32)).astype(jnp.bfloat16)
    hidden_grad = jnp.dot(cotangent, pruned_down.T, preferred_element_type=f32)
    gate_grad = (hidden_grad * up_val * logistic * (1.0 + gate_val * (1.0 - logistic))).astype(jnp.bfloat16)
    up_grad = (hidden_grad * gate_val * logistic).astype(jnp.bfloat16)
    grad_w_down = expand(jnp.dot(hidden.T, cotangent, preferred_element_type=f32), mask_down).astype(jnp.bfloat16)
    grad_w_gate = expand(jnp.dot(resid.T, gate_grad, preferred_element_type=f32), mask_gate).astype(jnp.bfloat16)
    grad_w_up = expand(jnp.dot(resid.T, up_grad, preferred_element_type=f32), mask_up).astype(jnp.bfloat16)
    grad_resid = (cotangent.astype(f32) + jnp.dot(gate_grad, pruned_gate.T, preferred_element_type=f32)
                  + jnp.dot(up_grad, pruned_up.T, preferred_element_type=f32)).astype(jnp.bfloat16)
    grad_attn = jnp.dot(grad_resid, pruned_out.T, preferred_element_type=f32).astype(jnp.bfloat16)
    grad_w_out = expand(jnp.dot(attn_out.T, grad_resid, preferred_element_type=f32), mask_out).astype(jnp.bfloat16)
    return (layer_out, grad_resid, grad_attn, grad_w_out, grad_w_gate, grad_w_up, grad_w_down)
```

```python
import jax
import jax.numpy as jnp
from jax import lax
from jax.sharding import PartitionSpec as P

BLOCK = 128
CHUNKS = 2


def expand(weight, flags):
    blocks_r = weight.shape[0] // BLOCK
    blocks_c = weight.shape[1] // BLOCK
    shaped = weight.reshape(blocks_r, BLOCK, blocks_c, BLOCK)
    return (shaped * flags.astype(weight.dtype)[:, None, :, None]).reshape(weight.shape)


def product_nn(left, right):
    return jnp.dot(left, right, preferred_element_type=jnp.float32)


def product_nt(left, right):
    return lax.dot_general(
        left, right, (((1,), (1,)), ((), ())), preferred_element_type=jnp.float32
    )


def product_tn(left, right):
    return lax.dot_general(
        left, right, (((0,), (0,)), ((), ())), preferred_element_type=jnp.float32
    )


def row_gather(value):
    return lax.all_gather(value, "row", axis=0, tiled=True)


def col_gather(value):
    return lax.all_gather(value, "col", axis=0, tiled=True)


def row_sum(panel):
    return lax.psum_scatter(panel.astype(jnp.bfloat16), "row", scatter_dimension=0, tiled=True)


def col_sum(panel):
    return lax.psum_scatter(panel, "col", scatter_dimension=0, tiled=True).astype(jnp.float32)


def after(value, *others):
    return lax.optimization_barrier((value,) + others)[0]


def local(
    resid_in,
    attn_out,
    cotangent,
    w_out,
    w_gate,
    w_up,
    w_down,
    mask_out,
    mask_gate,
    mask_up,
    mask_down,
):
    f32 = jnp.float32
    bf16 = jnp.bfloat16
    units = w_gate.shape[1]
    part = units // CHUNKS
    flag_part = part // BLOCK
    pruned_out = expand(w_out, mask_out)
    pruned_down = expand(w_down, mask_down)
    attn_full = row_gather(attn_out)
    upstream = col_gather(cotangent)
    projected = col_sum(product_nn(attn_full, pruned_out))
    hidden_part = product_nt(upstream, pruned_down).astype(bf16)
    hidden_grad = row_gather(row_sum(hidden_part))
    projected = after(projected, hidden_part)
    resid = (resid_in.astype(f32) + projected).astype(bf16)
    resid_full = col_gather(resid)
    resid_full = after(resid_full, hidden_grad)
    pairs, values = [], []
    for j in range(CHUNKS):
        cols = slice(j * part, (j + 1) * part)
        flags = slice(j * flag_part, (j + 1) * flag_part)
        pair = jnp.concatenate(
            [expand(w_gate[:, cols], mask_gate[:, flags]), expand(w_up[:, cols], mask_up[:, flags])], 1
        )
        pairs.append(pair)
        values.append(row_gather(row_sum(product_nn(resid_full, pair))))
    returned, lowered = 0.0, 0.0
    grads = []
    for j in range(CHUNKS):
        pair_val = values[j].astype(f32)
        gate_val, up_val = pair_val[:, :part], pair_val[:, part:]
        upper = hidden_grad[:, j * part : (j + 1) * part].astype(f32)
        logistic = jax.nn.sigmoid(gate_val)
        hidden = (gate_val * logistic * up_val).astype(bf16)
        gate_grad = (upper * up_val * logistic * (1.0 + gate_val * (1.0 - logistic))).astype(bf16)
        up_grad = (upper * gate_val * logistic).astype(bf16)
        grads.append((hidden, gate_grad, up_grad))
        returned = returned + product_nt(gate_grad, pairs[j][:, :part]) + product_nt(up_grad, pairs[j][:, part:])
        lowered = lowered + product_nn(hidden, pruned_down[j * part : (j + 1) * part])
    grad_resid = (cotangent.astype(f32) + col_sum(returned.astype(bf16))).astype(bf16)
    grad_full = col_gather(grad_resid)
    layer_out = (resid.astype(f32) + col_sum(after(lowered.astype(bf16), grad_full))).astype(bf16)
    grad_attn = row_sum(product_nt(grad_full, pruned_out))
    gates, ups, downs = [], [], []
    for j in range(CHUNKS):
        flags = slice(j * flag_part, (j + 1) * flag_part)
        hidden, gate_grad, up_grad = grads[j]
        gates.append(expand(product_tn(resid_full, gate_grad), mask_gate[:, flags]).astype(bf16))
        ups.append(expand(product_tn(resid_full, up_grad), mask_up[:, flags]).astype(bf16))
        downs.append(expand(product_tn(hidden, upstream), mask_down[flags]).astype(bf16))
    grad_w_gate = jnp.concatenate(gates, 1)
    grad_w_up = jnp.concatenate(ups, 1)
    grad_w_down = jnp.concatenate(downs, 0)
    grad_w_out = expand(product_tn(attn_full, grad_full), mask_out).astype(bf16)
    return (layer_out, grad_resid, grad_attn, grad_w_out, grad_w_gate, grad_w_up, grad_w_down)


def solution(mesh):
    placed = (
        P("col", "row"),
        P("row", "col"),
        P("col", "row"),
        P("col", "row"),
        P("row", "col"),
        P("row", "col"),
        P("col", "row"),
        P("col", "row"),
        P("row", "col"),
        P("row", "col"),
        P("col", "row"),
    )
    return jax.shard_map(
        local,
        mesh=mesh,
        in_specs=placed,
        out_specs=(
            P("col", "row"),
            P("col", "row"),
            P("row", "col"),
            P("col", "row"),
            P("row", "col"),
            P("row", "col"),
            P("col", "row"),
        ),
        check_vma=False,
    )
```

```python
import jax
import jax.numpy as jnp
from jax import lax
from jax.sharding import PartitionSpec as P

BLOCK = 128


def expand(weight, flags):
    blocks_r = weight.shape[0] // BLOCK
    blocks_c = weight.shape[1] // BLOCK
    shaped = weight.reshape(blocks_r, BLOCK, blocks_c, BLOCK)
    return (shaped * flags.astype(weight.dtype)[:, None, :, None]).reshape(weight.shape)


def product_nn(left, right):
    return jnp.dot(left, right, preferred_element_type=jnp.float32)


def product_nt(left, right):
    return lax.dot_general(
        left, right, (((1,), (1,)), ((), ())), preferred_element_type=jnp.float32
    )


def product_tn(left, right):
    return lax.dot_general(
        left, right, (((0,), (0,)), ((), ())), preferred_element_type=jnp.float32
    )


def row_gather(value):
    return lax.all_gather(value, "row", axis=0, tiled=True)


def col_gather(value):
    return lax.all_gather(value, "col", axis=0, tiled=True)


def row_swap(value, step):
    count = lax.axis_size("row")
    return lax.ppermute(value, "row", [(i, i ^ step) for i in range(count)])


def row_gather_direct(value):
    count = lax.axis_size("row")
    me = lax.axis_index("row")
    rows = value.shape[0]
    full = jnp.zeros((rows * count, value.shape[1]), value.dtype)
    for step in range(count):
        block = row_swap(value, step) if step else value
        full = lax.dynamic_update_slice(full, block, ((me ^ step) * rows, 0))
    return full


def row_sum_direct(panel):
    count = lax.axis_size("row")
    me = lax.axis_index("row")
    rows = panel.shape[0] // count
    total = 0.0
    for step in range(count):
        block = lax.dynamic_slice_in_dim(panel, (me ^ step) * rows, rows, 0)
        if step:
            block = row_swap(block, step)
        total = total + block.astype(jnp.float32)
    return total


def row_sum(panel):
    return lax.psum_scatter(panel, "row", scatter_dimension=0, tiled=True)


def col_sum(panel):
    return lax.psum_scatter(panel, "col", scatter_dimension=0, tiled=True).astype(jnp.float32)


def after(value, *others):
    return lax.optimization_barrier((value,) + others)[0]


def local(
    resid_in,
    attn_out,
    cotangent,
    w_out,
    w_gate,
    w_up,
    w_down,
    mask_out,
    mask_gate,
    mask_up,
    mask_down,
):
    f32 = jnp.float32
    bf16 = jnp.bfloat16
    units = w_gate.shape[1]
    width = w_down.shape[1]
    pruned_out = expand(w_out, mask_out)
    pruned_down = expand(w_down, mask_down)
    pair = jnp.concatenate([expand(w_gate, mask_gate), expand(w_up, mask_up)], 1)
    attn_full = row_gather_direct(attn_out)
    upstream = col_gather(cotangent)
    projected = col_sum(product_nn(attn_full, pruned_out))
    hidden_part = product_nt(upstream, pruned_down).astype(bf16)
    hidden_grad = row_sum_direct(hidden_part)
    projected = after(projected, hidden_part)
    resid = (resid_in.astype(f32) + projected).astype(bf16)
    resid_full = col_gather(resid)
    resid_full = after(resid_full, hidden_grad)
    pair_val = row_sum(product_nn(resid_full, pair).astype(bf16)).astype(f32)
    gate_val, up_val = pair_val[:, :units], pair_val[:, units:]
    logistic = jax.nn.sigmoid(gate_val)
    hidden = (gate_val * logistic * up_val).astype(bf16)
    gate_grad = (hidden_grad * up_val * logistic * (1.0 + gate_val * (1.0 - logistic))).astype(bf16)
    up_grad = (hidden_grad * gate_val * logistic).astype(bf16)
    full = row_gather(jnp.concatenate([gate_grad, up_grad, hidden], 1))
    pair_grad, hidden_full = full[:, : 2 * units], full[:, 2 * units :]
    returned = product_nt(pair_grad, pair).astype(bf16)
    lowered = product_nn(hidden_full, pruned_down).astype(bf16)
    both = col_sum(jnp.concatenate([returned, lowered], 1))
    grad_resid = (cotangent.astype(f32) + both[:, :width]).astype(bf16)
    layer_out = (resid.astype(f32) + both[:, width:]).astype(bf16)
    grad_full = col_gather(grad_resid)
    grad_attn = row_sum_direct(product_nt(grad_full, pruned_out).astype(bf16)).astype(bf16)
    grad_w_gate = expand(product_tn(resid_full, pair_grad[:, :units]), mask_gate).astype(bf16)
    grad_w_up = expand(product_tn(resid_full, pair_grad[:, units:]), mask_up).astype(bf16)
    grad_w_down = expand(product_tn(hidden_full, upstream), mask_down).astype(bf16)
    grad_w_out = expand(product_tn(attn_full, grad_full), mask_out).astype(bf16)
    return (layer_out, grad_resid, grad_attn, grad_w_out, grad_w_gate, grad_w_up, grad_w_down)


def solution(mesh):
    placed = (
        P("col", "row"),
        P("row", "col"),
        P("col", "row"),
        P("col", "row"),
        P("row", "col"),
        P("row", "col"),
        P("col", "row"),
        P("col", "row"),
        P("row", "col"),
        P("row", "col"),
        P("col", "row"),
    )
    return jax.shard_map(
        local,
        mesh=mesh,
        in_specs=placed,
        out_specs=(
            P("col", "row"),
            P("col", "row"),
            P("row", "col"),
            P("col", "row"),
            P("row", "col"),
            P("row", "col"),
            P("col", "row"),
        ),
        check_vma=False,
    )
```
